32 devices in a mesh: groups: 2 (over x), dp: 4 (over y, core), tensor: 4 (over z).
Axes of the slice: x: 2, y: 2, z: 4, core: 2. Of those that a mesh axis runs over, the one named last changes fastest.
Arguments:
- tokens: bfloat16 [16, 256, 4096], P(('groups', 'dp'), None, 'tensor'), parts along dimension 0, may hold values from -6 to 6
- ln_gain: float32 [4096], replicated, may hold values from 0.5 to 1.5
- w_query: bfloat16 [4096, 2048], P(None, 'tensor'), may hold values from -0.375 to 0.375
- w_key: bfloat16 [4096, 2048], P(None, 'tensor'), may hold values from -0.09375 to 0.09375
- w_value: bfloat16 [4096, 2048], P(None, 'tensor'), may hold values from -0.09375 to 0.09375
- w_out: bfloat16 [2048, 4096], P('tensor'), may hold values from -0.125 to 0.125
- final_gain: float32 [4096], replicated, may hold values from 0.5 to 1.5
- w_cross_key: bfloat16 [4096, 2048], P(None, 'tensor'), may hold values from -0.09375 to 0.09375
- w_cross_value: bfloat16 [4096, 2048], P(None, 'tensor'), may hold values from -0.09375 to 0.09375
- dec_query: bfloat16 [8, 32, 2048], P(('groups', 'dp'), None, 'tensor'), parts along dimension 0, may hold values from -24 to 24
- grad_out: bfloat16 [8, 32, 2048], P(('groups', 'dp'), None, 'tensor'), parts along dimension 0, may hold values from -6 to 6
- passage_query: int32 [16, 1], P('groups'), parts along dimension 0, may hold values from 0 to 3
- passage_length: int32 [16], P('groups'), parts along dimension 0, may hold values from 1 to 256, 1536 in all
Outputs:
- attended: bfloat16 [8, 32, 2048], P(('groups', 'dp'), None, 'tensor'), parts along dimension 0
- d_query: bfloat16 [8, 32, 2048], P(('groups', 'dp'), None, 'tensor'), parts along dimension 0
- d_values: bfloat16 [16, 256, 2048], P(('groups', 'dp'), None, 'tensor'), parts along dimension 0
The draws below stay inside these ranges and needn't reach their ends.
There are 2 independent parts, one for each index of `groups`. The reference program is written for one: setup_inputs(seed, part) draws one part's arguments, and reference() takes and returns one part's arrays. A program takes and returns all parts, laid end to end along the dimension named above; an argument that names none is the same for every part. Nothing has to cross between parts.
Inputs may be any that keep to these rules, and one draw needn't show every extreme that they name: `passage_query`: every query owns at least one passage.
All inputs are finite; a program needn't handle non-finite values.
Results may differ from the reference program's by a relative error of at most 0.04.
Values may be sent and summed in bfloat16 or wider, within the bound.
A program may use at most 128 MiB of HBM per device.

```python
import math
import jax
import jax.numpy as jnp
import numpy as np
from jax import lax

D = 4096
HEADS = 32
HD = 64
L = 256
DEC = 32
TP_HEADS = 8
HC = 2048
PASSAGES = 8
QUERIES = 4
N_TENSOR = 4


def draw_w_query(key, part):
    base = jax.random.truncated_normal(key, -6.0, 6.0, (D, HEADS * HD), jnp.float32) * D ** (-0.5)
    return base.astype(jnp.bfloat16)


def draw_dec_query(key, part):
    base = jax.random.truncated_normal(key, -6.0, 6.0, (QUERIES, DEC, HEADS * HD), jnp.float32)
    return base.astype(jnp.bfloat16)


def steps_of(stream_key, dims, split, smallest, top_value):
    loudness = 1.0
    for axis_at, blocks in split:
        heights = jax.random.uniform(jax.random.fold_in(jax.random.fold_in(stream_key, 6), axis_at), (blocks,), jnp.float32, smallest / len(split), top_value / len(split))
        loudness = loudness * jnp.repeat(jnp.exp(heights), dims[axis_at] // blocks).reshape((-1,) + (1,) * (len(dims) - 1 - axis_at))
    return loudness


def choose_distinct(own_key, rows, amount, top, lift):
    ranking = jax.random.permutation(jax.random.fold_in(own_key, 1), amount)
    favour = ranking
    for power in range(3):
        favour = favour * favour // amount
    favour = favour * lift // amount
    tickets = jax.random.randint(jax.random.fold_in(own_key, 2), (rows, amount), 0, 4096) + favour
    holders = jax.random.permutation(jax.random.fold_in(own_key, 3), rows)[jnp.arange(amount) % rows]
    tickets = jnp.where(jnp.arange(rows)[:, None] == holders[None, :], 1 << 14, tickets)
    priority = tickets * amount + jnp.arange(amount)
    return lax.top_k(priority.astype(jnp.int32), top)[1].astype(jnp.int32)


def profile(amount, total, limit, skew):
    portions = [(1 << 20) // math.isqrt(grade ** skew) + 1 for grade in range(2, amount + 1)]
    spare, given = total - limit - (amount - 1), [1] * (amount - 1)
    while spare > 0:
        free = [i for i in range(amount - 1) if given[i] < limit]
        whole, budget = sum([portions[i] for i in free]), spare
        for i in free:
            extra = min(limit - given[i], max(1, budget * portions[i] // whole), spare)
            given[i] = given[i] + extra
            spare = spare - extra
    return np.array([limit] + given)


def uneven(rng, amount, total, most, slope):
    if amount == 2:
        one = jax.random.randint(rng, (), max(1, total - most), min(most, total - 1) + 1)
        return jnp.stack([one, total - one])
    tallies = jnp.asarray(profile(amount, total, most, slope), jnp.int32)
    twos = (amount - 1) // 2
    giver, receiver = tallies[1:1 + 2 * twos:2], tallies[2:2 + 2 * twos:2]
    slack = jnp.minimum(giver - 1, most - receiver)
    shifted = jax.random.randint(jax.random.fold_in(rng, 1), (twos,), 0, 1 << 20) % (slack + 1)
    tallies = tallies.at[1:1 + 2 * twos:2].set(giver - shifted).at[2:2 + 2 * twos:2].set(receiver + shifted)
    return tallies[jax.random.permutation(jax.random.fold_in(rng, 2), amount)]


def normal_values(key, dims, width, reach, cuts=(), held_as=jnp.bfloat16):
    drawn = jax.random.normal(key, dims, jnp.float32) * width
    if len(cuts) > 0:
        drawn = steps_of(key, dims, cuts, -0.22, 0.18) * drawn
    return jnp.clip(drawn, min=-reach, max=reach).astype(held_as)


def setup_inputs(seed: int = 0, part: int = 0) -> dict:
    key_of = jax.random.split(jax.random.key(seed), 14)
    part_splits = jax.random.split(jax.random.fold_in(key_of[13], part), 14)
    return {
        "tokens": normal_values(part_splits[0], (PASSAGES, L, D), 1.0, 6.0, ((0, 4), (2, 4))),
        "ln_gain": jnp.clip(1.0 + 0.1 * jax.random.normal(key_of[1], (D,), jnp.float32), 0.5, 1.5),
        "w_query": draw_w_query(jax.random.fold_in(key_of[13], 71), part),
        "w_key": normal_values(key_of[3], (D, HC), D ** -0.5, 0.09375, ((1, 4),)),
        "w_value": normal_values(key_of[4], (D, HC), D ** -0.5, 0.09375, ((1, 4),)),
        "w_out": normal_values(key_of[5], (HC, D), HC ** -0.5, 0.125, ((0, 4),)),
        "final_gain": jnp.clip(1.0 + 0.1 * jax.random.normal(key_of[6], (D,), jnp.float32), 0.5, 1.5),
        "w_cross_key": normal_values(key_of[7], (D, HC), D ** -0.5, 0.09375, ((1, 4),)),
        "w_cross_value": normal_values(key_of[8], (D, HC), D ** -0.5, 0.09375, ((1, 4),)),
        "dec_query": draw_dec_query(jax.random.fold_in(jax.random.fold_in(key_of[13], part), 71), part),
        "grad_out": normal_values(part_splits[10], (QUERIES, DEC, HC), 1.0, 6.0, ((0, 4), (2, 4))),
        "passage_query": choose_distinct(part_splits[11], PASSAGES, QUERIES, 1, 4096),
        "passage_length": uneven(part_splits[12], PASSAGES, PASSAGES * L * 3 // 4, L, 1).astype(jnp.int32),
    }


blocked = -1e+30

def norm_rows(values, gain):
    return values * lax.rsqrt(lax.optimization_barrier(jnp.mean(values * values, axis=-1, keepdims=True)) + 1e-06) * gain

def reference(tokens, ln_gain, w_query, w_key, w_value, w_out, final_gain, w_cross_key, w_cross_value, dec_query, grad_out, passage_query, passage_length):
    score_scale = HD ** (-0.5)
    group_cols = TP_HEADS * HD
    flat_in = tokens.reshape(PASSAGES * L, D).astype(jnp.float32)
    normed = norm_rows(flat_in, ln_gain.astype(jnp.float32)).astype(jnp.bfloat16)

    def project(weight):
        return jnp.dot(normed, weight, preferred_element_type=jnp.float32).astype(jnp.bfloat16).reshape(PASSAGES, L, HEADS, HD)
    self_queries = project(w_query)
    self_keys = project(w_key)
    self_values = project(w_value)
    positions = jnp.arange(L, dtype=jnp.int32)
    valid = positions[None, :] < passage_length[:, None]

    def self_attend(packed):
        query_part, key_part, value_part, key_ok = packed
        scores = jnp.einsum('qhd,khd->hqk', query_part.astype(jnp.float32), key_part.astype(jnp.float32)) * score_scale
        scores = jnp.where(key_ok[None, None, :], scores, blocked)
        row_peak = lax.optimization_barrier(jnp.max(scores, axis=-1, keepdims=True))
        expd = jnp.where(key_ok[None, None, :], jnp.exp(scores - row_peak), 0.0)
        weights = (expd / lax.optimization_barrier(jnp.sum(expd, axis=-1, keepdims=True))).astype(jnp.bfloat16)
        return jnp.einsum('hqk,khd->qhd', weights.astype(jnp.float32), value_part.astype(jnp.float32)).astype(jnp.bfloat16)
    context = lax.map(self_attend, (self_queries, self_keys, self_values, valid)).reshape(PASSAGES * L, HC)
    mixed = jnp.zeros((PASSAGES * L, D), jnp.float32)
    for group in range(N_TENSOR):
        lower = group * group_cols
        term = jnp.dot(context[:, lower:lower + group_cols], w_out[lower:lower + group_cols], preferred_element_type=jnp.float32).astype(jnp.bfloat16)
        mixed = mixed + lax.optimization_barrier(term).astype(jnp.float32)
    hidden = flat_in + mixed
    encoded = norm_rows(hidden, final_gain.astype(jnp.float32)).astype(jnp.bfloat16)
    cross_keys = jnp.dot(encoded, w_cross_key, preferred_element_type=jnp.float32).astype(jnp.bfloat16).reshape(PASSAGES * L, HEADS, HD).astype(jnp.float32)
    cross_values = jnp.dot(encoded, w_cross_value, preferred_element_type=jnp.float32).astype(jnp.bfloat16).reshape(PASSAGES * L, HEADS, HD).astype(jnp.float32)
    token_query = jnp.repeat(passage_query[:, 0], L)
    token_valid = valid.reshape(-1)

    def per_query(carry, packed):
        query_id, query_rows, out_rows = packed
        key_mask = (token_query == query_id) & token_valid
        query_heads = query_rows.reshape(DEC, HEADS, HD).astype(jnp.float32)
        scores = jnp.einsum('ihd,thd->hit', query_heads, cross_keys) * score_scale
        scores = jnp.where(key_mask[None, None, :], scores, blocked)
        row_peak = lax.optimization_barrier(jnp.max(scores, axis=-1, keepdims=True))
        expd = jnp.where(key_mask[None, None, :], jnp.exp(scores - row_peak), 0.0)
        probs = expd / lax.optimization_barrier(jnp.sum(expd, axis=-1, keepdims=True))
        low = probs.astype(jnp.bfloat16)
        attended = jnp.einsum('hit,thd->ihd', low.astype(jnp.float32), cross_values).astype(jnp.bfloat16)
        out_grad = out_rows.reshape(DEC, HEADS, HD).astype(jnp.float32)
        row_delta = lax.optimization_barrier(jnp.sum(out_grad * attended.astype(jnp.float32), axis=-1))
        grad_probs = jnp.einsum('ihd,thd->hit', out_grad, cross_values)
        grad_scores = (probs * (grad_probs - row_delta.T[:, :, None])).astype(jnp.bfloat16)
        query_grad = (jnp.einsum('hit,thd->ihd', grad_scores.astype(jnp.float32), cross_keys) * score_scale).astype(jnp.bfloat16)
        carry = carry + jnp.einsum('hit,ihd->thd', low.astype(jnp.float32), out_grad)
        return (carry, (attended.reshape(DEC, HC), query_grad.reshape(DEC, HC)))
    start_sum = jnp.zeros((PASSAGES * L, HEADS, HD), jnp.float32)
    value_sum, outputs = lax.scan(per_query, start_sum, (jnp.arange(QUERIES, dtype=jnp.int32), dec_query, grad_out))
    d_values = value_sum.astype(jnp.bfloat16).reshape(PASSAGES, L, HC)
    return (outputs[0], outputs[1], d_values)
```

```python
import jax
import jax.numpy as jnp
from jax import lax
from jax.sharding import PartitionSpec as P

HD = 64


blocked = -1e30


def norm_rows(values, gain):
    return values * lax.rsqrt(jnp.mean(values * values, axis=-1, keepdims=True) + 1e-06) * gain


def shards(
    tokens,
    ln_gain,
    w_query,
    w_key,
    w_value,
    w_out,
    final_gain,
    w_cross_key,
    w_cross_value,
    dec_query,
    grad_out,
    passage_query,
    passage_length,
):
    pass_dev, seq_len, part_width = tokens.shape
    local_cols = w_query.shape[1]
    local_heads = local_cols // HD
    score_scale = HD ** (-0.5)
    row_count = pass_dev * seq_len
    query_count = dec_query.shape[0]
    dec_len = dec_query.shape[1]
    slices = lax.axis_size("groups") * lax.axis_size("dp")
    slice_rows = local_cols // slices
    slice_at = lax.axis_index("groups") * lax.axis_size("dp") + lax.axis_index("dp")
    out_slice = lax.dynamic_slice_in_dim(w_out, slice_at * slice_rows, slice_rows, 0)
    out_slice = lax.all_gather(out_slice, "tensor", axis=0, tiled=True)
    out_full = lax.all_gather(out_slice, ("groups", "dp"), axis=0, tiled=True)
    asked = lax.all_gather(jnp.stack([dec_query, grad_out]), "dp", axis=1, tiled=True)
    gathered_in = lax.all_gather(tokens, "tensor", axis=2, tiled=True)
    full_width = gathered_in.shape[2]
    inputs_f = gathered_in.reshape(row_count, full_width).astype(jnp.float32)
    normed = norm_rows(inputs_f, ln_gain).astype(jnp.bfloat16)

    def project(weight):
        return (
            jnp.dot(normed, weight, preferred_element_type=jnp.float32)
            .astype(jnp.bfloat16)
            .reshape(pass_dev, seq_len, local_heads, HD)
        )

    self_queries = project(w_query)
    self_keys = project(w_key)
    self_values = project(w_value)
    pass_start = lax.axis_index("dp") * pass_dev
    own_length = lax.dynamic_slice_in_dim(passage_length, pass_start, pass_dev)
    positions = jnp.arange(seq_len, dtype=jnp.int32)
    own_valid = positions[None, :] < own_length[:, None]
    scores = (
        jnp.einsum("pqhd,pkhd->phqk", self_queries, self_keys, preferred_element_type=jnp.float32)
        * score_scale
    )
    scores = jnp.where(own_valid[:, None, None, :], scores, blocked)
    row_peak = jnp.max(scores, axis=-1, keepdims=True)
    expd = jnp.where(own_valid[:, None, None, :], jnp.exp(scores - row_peak), 0.0)
    weights = (expd / jnp.sum(expd, axis=-1, keepdims=True)).astype(jnp.bfloat16)
    context = (
        jnp.einsum("phqk,pkhd->pqhd", weights, self_values, preferred_element_type=jnp.float32)
        .astype(jnp.bfloat16)
        .reshape(row_count, local_cols)
    )
    all_context = lax.all_gather(context, "tensor", axis=0, tiled=False)
    tensor_count = all_context.shape[0]
    all_context = (
        all_context.reshape(tensor_count, row_count, slices, slice_rows)
        .transpose(1, 2, 0, 3)
        .reshape(row_count, tensor_count * local_cols)
    )
    summed = jnp.dot(all_context, out_full, preferred_element_type=jnp.float32)
    encoded = norm_rows(inputs_f + summed, final_gain).astype(jnp.bfloat16)
    cross_keys = jnp.dot(encoded, w_cross_key, preferred_element_type=jnp.float32).astype(
        jnp.bfloat16
    )
    cross_values = jnp.dot(encoded, w_cross_value, preferred_element_type=jnp.float32).astype(
        jnp.bfloat16
    )
    own_query = lax.dynamic_slice_in_dim(passage_query[:, 0], pass_start, pass_dev)
    chosen = own_query[:, None] == jnp.arange(asked.shape[1], dtype=jnp.int32)[None, :]
    picked = jnp.sum(
        jnp.where(chosen[None, :, :, None, None], asked[:, None].astype(jnp.float32), 0.0), axis=2
    ).astype(jnp.bfloat16)
    picked = picked.reshape(2, pass_dev, dec_len, local_heads, HD)
    query_heads, out_grad = picked[0], picked[1]
    key_heads = cross_keys.reshape(pass_dev, seq_len, local_heads, HD)
    value_heads = cross_values.reshape(pass_dev, seq_len, local_heads, HD)
    key_ok = own_valid[:, None, None, :]
    cross_scores = (
        jnp.einsum("pihd,pthd->phit", query_heads, key_heads, preferred_element_type=jnp.float32)
        * score_scale
    )
    cross_scores = jnp.where(key_ok, cross_scores, blocked)
    own_peak = jnp.max(cross_scores, axis=-1, keepdims=True)
    own_exp = jnp.where(key_ok, jnp.exp(cross_scores - own_peak), 0.0)
    own_sum = jnp.sum(own_exp, axis=-1, keepdims=True)
    own_probs = own_exp / own_sum
    grad_probs = jnp.einsum(
        "pihd,pthd->phit", out_grad, value_heads, preferred_element_type=jnp.float32
    )
    own_delta = jnp.sum(own_probs * grad_probs, axis=-1, keepdims=True)
    stats = jnp.concatenate([own_peak, own_sum, own_delta], axis=-1)
    all_stats = lax.all_gather(stats, "dp", axis=0, tiled=True)
    own_low = own_probs.astype(jnp.bfloat16)
    centred = (own_probs * (grad_probs - own_delta)).astype(jnp.bfloat16)

    def over_keys(factor, heads):
        return jnp.einsum("phit,pthd->pihd", factor, heads, preferred_element_type=jnp.float32)

    partials = jnp.stack(
        [
            over_keys(own_low, value_heads),
            over_keys(centred, key_heads),
            over_keys(own_low, key_heads),
        ],
        axis=1,
    ).astype(jnp.bfloat16)
    partials = partials.reshape(pass_dev, 3, dec_len, local_cols)
    all_partials = lax.all_gather(partials, "dp", axis=0, tiled=True)
    pass_total = all_partials.shape[0]

    def shares(targets):
        owned = (targets[:, None] == passage_query[:, 0][None, :])[:, :, None, None]
        peaks = jnp.where(owned, all_stats[None, :, :, :, 0], blocked)
        top = jnp.max(peaks, axis=1, keepdims=True)
        raised = jnp.where(owned, jnp.exp(peaks - top) , 0.0)
        total = jnp.sum(raised * all_stats[None, :, :, :, 1], axis=1, keepdims=True)
        return raised, total, top

    _, own_total, own_top = shares(own_query)
    low = (
        own_exp * (jnp.exp(own_peak - own_top[:, 0, :, :, None]) / own_total[:, 0, :, :, None])
    ).astype(jnp.bfloat16)
    d_values = jnp.einsum(
        "phit,pihd->pthd", low, out_grad, preferred_element_type=jnp.float32
    ).astype(jnp.bfloat16).reshape(pass_dev, seq_len, local_cols)
    query_ids = lax.axis_index("dp") * query_count + jnp.arange(query_count, dtype=jnp.int32)
    raised, total, _ = shares(query_ids)
    share = raised * all_stats[None, :, :, :, 1] / total
    share = share.transpose(0, 1, 3, 2)[..., None]
    pieces = all_partials.astype(jnp.float32).reshape(
        1, pass_total, 3, dec_len, local_heads, HD
    )
    attended_heads = jnp.sum(share * pieces[:, :, 0], axis=1).astype(jnp.bfloat16)
    grad_heads = grad_out.reshape(query_count, dec_len, local_heads, HD)
    row_delta = jnp.sum(
        grad_heads.astype(jnp.float32) * attended_heads.astype(jnp.float32), axis=-1
    )
    shift = all_stats[None, :, :, :, 2].transpose(0, 1, 3, 2) - row_delta[:, None]
    query_term = jnp.sum(share * (pieces[:, :, 1] + shift[..., None] * pieces[:, :, 2]), axis=1)
    attended = attended_heads.reshape(query_count, dec_len, local_cols)
    d_query = (
        (query_term * score_scale).astype(jnp.bfloat16).reshape(query_count, dec_len, local_cols)
    )
    return (attended, d_query, d_values)


def solution(mesh):
    in_specs = (
        P(("groups", "dp"), None, "tensor"),
        P(),
        P(None, "tensor"),
        P(None, "tensor"),
        P(None, "tensor"),
        P("tensor", None),
        P(),
        P(None, "tensor"),
        P(None, "tensor"),
        P(("groups", "dp"), None, "tensor"),
        P(("groups", "dp"), None, "tensor"),
        P("groups", None),
        P("groups"),
    )
    out_specs = (
        P(("groups", "dp"), None, "tensor"),
        P(("groups", "dp"), None, "tensor"),
        P(("groups", "dp"), None, "tensor"),
    )
    return jax.shard_map(shards, mesh=mesh, in_specs=in_specs, out_specs=out_specs, check_vma=False)
```

```python
import functools

import jax
import jax.numpy as jnp
from jax import lax
from jax.experimental import pallas as pl
from jax.experimental.pallas import tpu as pltpu
from jax.sharding import PartitionSpec as P

HD = 64


blocked = -1e30


def norm_rows(values, gain):
    return values * lax.rsqrt(jnp.mean(values * values, axis=-1, keepdims=True) + 1e-06) * gain


MESH = pl.DeviceIdType.MESH


def remote(src, dst, send_sem, recv_sem, target):
    return pltpu.make_async_remote_copy(
        src_ref=src,
        dst_ref=dst,
        send_sem=send_sem,
        recv_sem=recv_sem,
        device_id=target,
        device_id_type=MESH,
    )


def greet(targets, conditions):
    barrier = pltpu.get_barrier_semaphore()
    amount = 0
    for target, condition in zip(targets, conditions):
        if condition is None:
            pl.semaphore_signal(barrier, inc=1, device_id=target, device_id_type=MESH)
            amount = amount + 1
        else:

            @pl.when(condition)
            def _(target=target):
                pl.semaphore_signal(barrier, inc=1, device_id=target, device_id_type=MESH)

            amount = amount + condition.astype(jnp.int32)
    pl.semaphore_wait(barrier, amount)


class Chain:
    def __init__(self, count, place, own, block, send_sem, recv_sem):
        self.count, self.place, self.own, self.block = count, place, own, block
        self.send_sem, self.recv_sem = send_sem, recv_sem

    def arriving(self, step, way):
        index = self.place - 1 - step if way == 0 else self.place + 1 + step
        return index, (index >= 0 if way == 0 else index < self.count)

    def onward(self, way):
        target = self.place + 1 if way == 0 else self.place - 1
        return target, (target < self.count if way == 0 else target >= 0)

    def copy(self, step, way, index, src=None):
        block = self.block(index)
        target, _ = self.onward(way)
        slot = 2 * step + way
        return remote(
            block if src is None else src,
            block,
            self.send_sem.at[slot],
            self.recv_sem.at[slot],
            {"tensor": target},
        )

    def begin(self):
        for way in range(2):

            @pl.when(self.onward(way)[1])
            def _(way=way):
                self.copy(0, way, self.place, self.own).start()

    def receive(self, step, way):
        index, _ = self.arriving(step, way)
        self.copy(step, way, index).wait_recv()
        if step + 1 < self.count - 1:

            @pl.when(self.onward(way)[1])
            def _():
                self.copy(step + 1, way, index).start()

    def finish(self):
        for step in range(self.count - 1):
            for way in range(2):
                index = self.place - step if way == 0 else self.place + step
                there = index >= 0 if way == 0 else index < self.count

                @pl.when(there & self.onward(way)[1])
                def _(step=step, way=way, index=index):
                    self.copy(step, way, index, self.own if step == 0 else None).wait_send()


def columns(ref, index, width):
    return ref.at[:, pl.ds(pl.multiple_of(index * width, width), width)]


def line_targets(count, place):
    return [{"tensor": place + 1}, {"tensor": place - 1}], [place + 1 < count, place >= 1]


def line_kernel(count, x_ref, out_ref, local_sem, send_sem, recv_sem):
    place = lax.axis_index("tensor")
    width = x_ref.shape[1]
    keep = pltpu.make_async_copy(x_ref, columns(out_ref, place, width), local_sem)
    keep.start()
    greet(*line_targets(count, place))
    chain = Chain(
        count, place, x_ref, lambda index: columns(out_ref, index, width), send_sem, recv_sem
    )
    chain.begin()
    for step in range(count - 1):
        for way in range(2):

            @pl.when(chain.arriving(step, way)[1])
            def _(step=step, way=way):
                chain.receive(step, way)

    chain.finish()
    keep.wait()


def line_gather(x, count):
    slots = 2 * (count - 1)
    return pl.pallas_call(
        functools.partial(line_kernel, count),
        out_shape=jax.ShapeDtypeStruct((x.shape[0], x.shape[1] * count), x.dtype),
        in_specs=[pl.BlockSpec(memory_space=pl.ANY)],
        out_specs=pl.BlockSpec(memory_space=pl.ANY),
        scratch_shapes=[
            pltpu.SemaphoreType.DMA,
            pltpu.SemaphoreType.DMA((slots,)),
            pltpu.SemaphoreType.DMA((slots,)),
        ],
        compiler_params=pltpu.CompilerParams(collective_id=1, has_side_effects=True),
    )(x)


def spread_kernel(
    sizes,
    tok_ref,
    w_ref,
    tok_out,
    w_out,
    local_sem,
    tok_send,
    tok_recv,
    w_send,
    w_recv,
    g_send,
    g_recv,
    y_send,
    y_recv,
    c_send,
    c_recv,
):
    groups, rows, count = sizes
    group, dp, place = (lax.axis_index(name) for name in ("groups", "dp", "tensor"))
    row, core = lax.div(dp, 2), lax.rem(dp, 2)
    width = tok_ref.shape[1]
    keeps = (
        pltpu.make_async_copy(tok_ref, columns(tok_out, place, width), local_sem.at[0]),
        pltpu.make_async_copy(w_ref, w_out.at[place], local_sem.at[1]),
    )
    for keep in keeps:
        keep.start()
    other_groups = [lax.rem(group + hop, groups) for hop in range(groups)]
    other_rows = [lax.rem(row + hop, rows) for hop in range(rows)]
    sibling = {"dp": row * 2 + 1 - core}
    targets, conditions = line_targets(count, place)
    targets += [{"groups": g} for g in other_groups[1:]]
    targets += [{"dp": y * 2 + core} for y in other_rows[1:]] + [sibling]
    greet(targets, conditions + [None] * (groups + rows - 1))

    def at(group_at, row_at, core_at):
        return (group_at * rows + row_at) * 2 + core_at

    mine = at(group, row, core)
    weights = Chain(
        count, place, w_ref.at[mine], lambda index: w_out.at[index, mine], w_send, w_recv
    )
    toks = Chain(
        count, place, tok_ref, lambda index: columns(tok_out, index, width), tok_send, tok_recv
    )

    def across(step, way, hop, outward):
        index, slot = weights.arriving(step, way)[0], 2 * step + way
        sems = g_send.at[slot, hop - 1], g_recv.at[slot, hop - 1]
        there = w_out.at[index, mine]
        source = at(other_groups[groups - hop], row, core)
        here = w_out.at[index, source]
        target = {"groups": other_groups[hop]}
        block = there if outward else here
        return remote(block, block, *sems, target)

    def along(step, way, hop_g, hop, outward):
        index, slot = weights.arriving(step, way)[0], 2 * step + way
        sems = y_send.at[slot, hop_g, hop - 1], y_recv.at[slot, hop_g, hop - 1]
        block_group = other_groups[(groups - hop_g) % groups]
        there = w_out.at[index, at(block_group, row, core)]
        here = w_out.at[index, at(block_group, other_rows[rows - hop], core)]
        target = {"dp": other_rows[hop] * 2 + core}
        block = there if outward else here
        return remote(block, block, *sems, target)

    def beside(step, way, hop_g, hop, outward):
        index, slot = weights.arriving(step, way)[0], 2 * step + way
        sems = c_send.at[slot, hop_g, hop], c_recv.at[slot, hop_g, hop]
        block_group = other_groups[(groups - hop_g) % groups]
        block_row = other_rows[(rows - hop) % rows]
        there = w_out.at[index, at(block_group, block_row, core)]
        here = w_out.at[index, at(block_group, block_row, 1 - core)]
        block = there if outward else here
        return remote(block, block, *sems, sibling)

    def first(step, way):
        weights.receive(step, way)
        for hop in range(1, groups):
            across(step, way, hop, True).start()
        for hop in range(1, rows):
            along(step, way, 0, hop, True).start()
        beside(step, way, 0, 0, True).start()

    def second(step, way):
        for hop_g in range(1, groups):
            across(step, way, hop_g, False).wait_recv()
            for hop in range(1, rows):
                along(step, way, hop_g, hop, True).start()
            beside(step, way, hop_g, 0, True).start()

    def third(step, way):
        for hop_g in range(groups):
            for hop in range(1, rows):
                along(step, way, hop_g, hop, False).wait_recv()
                beside(step, way, hop_g, hop, True).start()

    def last(step, way):
        for hop_g in range(groups):
            for hop in range(rows):
                beside(step, way, hop_g, hop, False).wait_recv()
        for hop in range(1, groups):
            across(step, way, hop, True).wait_send()
        for hop_g in range(groups):
            for hop in range(1, rows):
                along(step, way, hop_g, hop, True).wait_send()
            for hop in range(rows):
                beside(step, way, hop_g, hop, True).wait_send()

    def each_way(step, act):
        for way in range(2):

            @pl.when(weights.arriving(step, way)[1])
            def _(way=way):
                act(step, way)

    weights.begin()
    toks.begin()
    for step in range(count - 1):
        each_way(step, first)
        if step >= 1:
            each_way(step - 1, second)
        each_way(step, toks.receive)
        if step >= 1:
            each_way(step - 1, third)
    each_way(count - 2, second)
    each_way(count - 2, third)
    for step in range(count - 1):
        each_way(step, last)
    weights.finish()
    toks.finish()
    for keep in keeps:
        keep.wait()


def spread(tokens, w_slices, groups, rows, count):
    slots = 2 * (count - 1)
    sems = [(slots,), (slots,), (slots, groups - 1), (slots, groups, rows - 1)]
    sems.append((slots, groups, rows))
    return pl.pallas_call(
        functools.partial(spread_kernel, (groups, rows, count)),
        out_shape=(
            jax.ShapeDtypeStruct((tokens.shape[0], tokens.shape[1] * count), tokens.dtype),
            jax.ShapeDtypeStruct((count,) + w_slices.shape, w_slices.dtype),
        ),
        in_specs=[pl.BlockSpec(memory_space=pl.ANY)] * 2,
        out_specs=(pl.BlockSpec(memory_space=pl.ANY),) * 2,
        scratch_shapes=[pltpu.SemaphoreType.DMA((2,))]
        + [pltpu.SemaphoreType.DMA(shape) for shape in sems for _ in range(2)],
        compiler_params=pltpu.CompilerParams(collective_id=0, has_side_effects=True),
    )(tokens, w_slices)


def shards(
    tokens,
    ln_gain,
    w_query,
    w_key,
    w_value,
    w_out,
    final_gain,
    w_cross_key,
    w_cross_value,
    dec_query,
    grad_out,
    passage_query,
    passage_length,
):
    pass_dev, seq_len, part_width = tokens.shape
    local_cols = w_query.shape[1]
    local_heads = local_cols // HD
    score_scale = HD ** (-0.5)
    row_count = pass_dev * seq_len
    query_count = dec_query.shape[0]
    dec_len = dec_query.shape[1]
    groups, dp_count = lax.axis_size("groups"), lax.axis_size("dp")
    tensor_count = lax.axis_size("tensor")
    asked = lax.all_gather(jnp.stack([dec_query, grad_out]), "dp", axis=1, tiled=True)
    gathered_in, out_full = spread(
        tokens.reshape(row_count, part_width),
        w_out.reshape(groups * dp_count, local_cols // (groups * dp_count), w_out.shape[1]),
        groups,
        dp_count // 2,
        tensor_count,
    )
    full_width = gathered_in.shape[1]
    out_full = out_full.reshape(tensor_count * local_cols, full_width)
    inputs_f = gathered_in.reshape(row_count, full_width).astype(jnp.float32)
    normed = norm_rows(inputs_f, ln_gain).astype(jnp.bfloat16)

    def project(weight):
        return (
            jnp.dot(normed, weight, preferred_element_type=jnp.float32)
            .astype(jnp.bfloat16)
            .reshape(pass_dev, seq_len, local_heads, HD)
        )

    self_queries = project(w_query)
    self_keys = project(w_key)
    self_values = project(w_value)
    pass_start = lax.axis_index("dp") * pass_dev
    own_length = lax.dynamic_slice_in_dim(passage_length, pass_start, pass_dev)
    positions = jnp.arange(seq_len, dtype=jnp.int32)
    own_valid = positions[None, :] < own_length[:, None]
    scores = (
        jnp.einsum("pqhd,pkhd->phqk", self_queries, self_keys, preferred_element_type=jnp.float32)
        * score_scale
    )
    scores = jnp.where(own_valid[:, None, None, :], scores, blocked)
    row_peak = jnp.max(scores, axis=-1, keepdims=True)
    expd = jnp.where(own_valid[:, None, None, :], jnp.exp(scores - row_peak), 0.0)
    weights = (expd / jnp.sum(expd, axis=-1, keepdims=True)).astype(jnp.bfloat16)
    context = (
        jnp.einsum("phqk,pkhd->pqhd", weights, self_values, preferred_element_type=jnp.float32)
        .astype(jnp.bfloat16)
        .reshape(row_count, local_cols)
    )
    all_context = line_gather(context, tensor_count)
    summed = jnp.dot(all_context, out_full, preferred_element_type=jnp.float32)
    encoded = norm_rows(inputs_f + summed, final_gain).astype(jnp.bfloat16)
    cross_keys = jnp.dot(encoded, w_cross_key, preferred_element_type=jnp.float32).astype(
        jnp.bfloat16
    )
    cross_values = jnp.dot(encoded, w_cross_value, preferred_element_type=jnp.float32).astype(
        jnp.bfloat16
    )
    own_query = lax.dynamic_slice_in_dim(passage_query[:, 0], pass_start, pass_dev)
    chosen = own_query[:, None] == jnp.arange(asked.shape[1], dtype=jnp.int32)[None, :]
    picked = jnp.sum(
        jnp.where(chosen[None, :, :, None, None], asked[:, None].astype(jnp.float32), 0.0), axis=2
    ).astype(jnp.bfloat16)
    picked = picked.reshape(2, pass_dev, dec_len, local_heads, HD)
    query_heads, out_grad = picked[0], picked[1]
    key_heads = cross_keys.reshape(pass_dev, seq_len, local_heads, HD)
    value_heads = cross_values.reshape(pass_dev, seq_len, local_heads, HD)
    key_ok = own_valid[:, None, None, :]
    cross_scores = (
        jnp.einsum("pihd,pthd->phit", query_heads, key_heads, preferred_element_type=jnp.float32)
        * score_scale
    )
    cross_scores = jnp.where(key_ok, cross_scores, blocked)
    own_peak = jnp.max(cross_scores, axis=-1, keepdims=True)
    own_exp = jnp.where(key_ok, jnp.exp(cross_scores - own_peak), 0.0)
    own_sum = jnp.sum(own_exp, axis=-1, keepdims=True)
    own_probs = own_exp / own_sum
    grad_probs = jnp.einsum(
        "pihd,pthd->phit", out_grad, value_heads, preferred_element_type=jnp.float32
    )
    own_delta = jnp.sum(own_probs * grad_probs, axis=-1, keepdims=True)
    stats = jnp.concatenate([own_peak, own_sum, own_delta], axis=-1)
    all_stats = lax.all_gather(stats, "dp", axis=0, tiled=True)
    own_low = own_probs.astype(jnp.bfloat16)
    centred = (own_probs * (grad_probs - own_delta)).astype(jnp.bfloat16)

    def over_keys(factor, heads):
        return jnp.einsum("phit,pthd->pihd", factor, heads, preferred_element_type=jnp.float32)

    partials = jnp.stack(
        [
            over_keys(own_low, value_heads),
            over_keys(centred, key_heads),
            over_keys(own_low, key_heads),
        ],
        axis=1,
    ).astype(jnp.bfloat16)
    partials = partials.reshape(pass_dev, 3, dec_len, local_cols)
    all_partials = lax.all_gather(partials, "dp", axis=0, tiled=True)
    pass_total = all_partials.shape[0]

    def shares(targets):
        owned = (targets[:, None] == passage_query[:, 0][None, :])[:, :, None, None]
        peaks = jnp.where(owned, all_stats[None, :, :, :, 0], blocked)
        top = jnp.max(peaks, axis=1, keepdims=True)
        raised = jnp.where(owned, jnp.exp(peaks - top) , 0.0)
        total = jnp.sum(raised * all_stats[None, :, :, :, 1], axis=1, keepdims=True)
        return raised, total, top

    _, own_total, own_top = shares(own_query)
    low = (
        own_exp * (jnp.exp(own_peak - own_top[:, 0, :, :, None]) / own_total[:, 0, :, :, None])
    ).astype(jnp.bfloat16)
    d_values = jnp.einsum(
        "phit,pihd->pthd", low, out_grad, preferred_element_type=jnp.float32
    ).astype(jnp.bfloat16).reshape(pass_dev, seq_len, local_cols)
    query_ids = lax.axis_index("dp") * query_count + jnp.arange(query_count, dtype=jnp.int32)
    raised, total, _ = shares(query_ids)
    share = raised * all_stats[None, :, :, :, 1] / total
    share = share.transpose(0, 1, 3, 2)[..., None]
    pieces = all_partials.astype(jnp.float32).reshape(
        1, pass_total, 3, dec_len, local_heads, HD
    )
    attended_heads = jnp.sum(share * pieces[:, :, 0], axis=1).astype(jnp.bfloat16)
    grad_heads = grad_out.reshape(query_count, dec_len, local_heads, HD)
    row_delta = jnp.sum(
        grad_heads.astype(jnp.float32) * attended_heads.astype(jnp.float32), axis=-1
    )
    shift = all_stats[None, :, :, :, 2].transpose(0, 1, 3, 2) - row_delta[:, None]
    query_term = jnp.sum(share * (pieces[:, :, 1] + shift[..., None] * pieces[:, :, 2]), axis=1)
    attended = attended_heads.reshape(query_count, dec_len, local_cols)
    d_query = (
        (query_term * score_scale).astype(jnp.bfloat16).reshape(query_count, dec_len, local_cols)
    )
    return (attended, d_query, d_values)


def solution(mesh):
    in_specs = (
        P(("groups", "dp"), None, "tensor"),
        P(),
        P(None, "tensor"),
        P(None, "tensor"),
        P(None, "tensor"),
        P("tensor", None),
        P(),
        P(None, "tensor"),
        P(None, "tensor"),
        P(("groups", "dp"), None, "tensor"),
        P(("groups", "dp"), None, "tensor"),
        P("groups", None),
        P("groups"),
    )
    out_specs = (
        P(("groups", "dp"), None, "tensor"),
        P(("groups", "dp"), None, "tensor"),
        P(("groups", "dp"), None, "tensor"),
    )
    return jax.shard_map(shards, mesh=mesh, in_specs=in_specs, out_specs=out_specs, check_vma=False)
```

```python
import functools

import jax
import jax.numpy as jnp
from jax import lax
from jax.experimental import pallas as pl
from jax.experimental.pallas import tpu as pltpu
from jax.sharding import PartitionSpec as P

HD = 64


blocked = -1e30


def norm_rows(values, gain):
    return values * lax.rsqrt(jnp.mean(values * values, axis=-1, keepdims=True) + 1e-06) * gain


MESH = pl.DeviceIdType.MESH


def remote(src, dst, send_sem, recv_sem, target):
    return pltpu.make_async_remote_copy(
        src_ref=src,
        dst_ref=dst,
        send_sem=send_sem,
        recv_sem=recv_sem,
        device_id=target,
        device_id_type=MESH,
    )


def greet(targets, conditions):
    barrier = pltpu.get_barrier_semaphore()
    amount = 0
    for target, condition in zip(targets, conditions):
        if condition is None:
            pl.semaphore_signal(barrier, inc=1, device_id=target, device_id_type=MESH)
            amount = amount + 1
        else:

            @pl.when(condition)
            def _(target=target):
                pl.semaphore_signal(barrier, inc=1, device_id=target, device_id_type=MESH)

            amount = amount + condition.astype(jnp.int32)
    pl.semaphore_wait(barrier, amount)


class Chain:
    def __init__(self, count, place, parts, own, block, send_sem, recv_sem):
        self.count, self.place, self.parts = count, place, parts
        self.own, self.block = own, block
        self.send_sem, self.recv_sem = send_sem, recv_sem

    def arriving(self, step, way):
        index = self.place - 1 - step if way == 0 else self.place + 1 + step
        return index, (index >= 0 if way == 0 else index < self.count)

    def onward(self, way):
        target = self.place + 1 if way == 0 else self.place - 1
        return target, (target < self.count if way == 0 else target >= 0)

    def copy(self, step, way, index, part, first=False):
        block = self.block(index, part)
        slot = 2 * step + way
        return remote(
            self.own(part) if first else block,
            block,
            self.send_sem.at[slot, part],
            self.recv_sem.at[slot, part],
            {"tensor": self.onward(way)[0]},
        )

    def begin(self):
        for part in range(self.parts):
            for way in range(2):

                @pl.when(self.onward(way)[1])
                def _(way=way, part=part):
                    self.copy(0, way, self.place, part, True).start()

    def receive(self, step, part):
        for way in range(2):
            index, there = self.arriving(step, way)

            @pl.when(there)
            def _(way=way, index=index):
                self.copy(step, way, index, part).wait_recv()
                if step + 1 < self.count - 1:

                    @pl.when(self.onward(way)[1])
                    def _():
                        self.copy(step + 1, way, index, part).start()

    def finish(self):
        for step in range(self.count - 1):
            for way in range(2):
                index = self.place - step if way == 0 else self.place + step
                there = index >= 0 if way == 0 else index < self.count

                @pl.when(there & self.onward(way)[1])
                def _(step=step, way=way, index=index):
                    for part in range(self.parts):
                        self.copy(step, way, index, part, step == 0).wait_send()


PARTS = 2


def parted(ref, parts, part):
    rows = ref.shape[0] // parts
    return ref.at[pl.ds(part * rows, rows)]


def part_columns(ref, index, width, parts, part):
    rows = ref.shape[0] // parts
    return ref.at[
        pl.ds(part * rows, rows), pl.ds(pl.multiple_of(index * width, width), width)
    ]


def columns(ref, index, width):
    return ref.at[:, pl.ds(pl.multiple_of(index * width, width), width)]


def line_targets(count, place):
    return [{"tensor": place + 1}, {"tensor": place - 1}], [place + 1 < count, place >= 1]


def line_kernel(count, x_ref, out_ref, local_sem, send_sem, recv_sem):
    place = lax.axis_index("tensor")
    width = x_ref.shape[1]
    keep = pltpu.make_async_copy(x_ref, columns(out_ref, place, width), local_sem)
    keep.start()
    greet(*line_targets(count, place))
    chain = Chain(
        count,
        place,
        PARTS,
        lambda part: parted(x_ref, PARTS, part),
        lambda index, part: part_columns(out_ref, index, width, PARTS, part),
        send_sem,
        recv_sem,
    )
    chain.begin()
    for step in range(count - 1):
        for part in range(PARTS):
            chain.receive(step, part)
    chain.finish()
    keep.wait()


def line_gather(x, count, collective_id):
    slots = 2 * (count - 1)
    return pl.pallas_call(
        functools.partial(line_kernel, count),
        out_shape=jax.ShapeDtypeStruct((x.shape[0], x.shape[1] * count), x.dtype),
        in_specs=[pl.BlockSpec(memory_space=pl.ANY)],
        out_specs=pl.BlockSpec(memory_space=pl.ANY),
        scratch_shapes=[
            pltpu.SemaphoreType.DMA,
            pltpu.SemaphoreType.DMA((slots, PARTS)),
            pltpu.SemaphoreType.DMA((slots, PARTS)),
        ],
        compiler_params=pltpu.CompilerParams(collective_id=collective_id, has_side_effects=True),
    )(x)


def plane_kernel(
    sizes,
    tok_ref,
    w_ref,
    got_ref,
    tok_out,
    w_out,
    staged,
    held,
    local_sem,
    tok_send,
    tok_recv,
    g_send,
    g_recv,
    y_send,
    y_recv,
    c_send,
    c_recv,
):
    groups, rows, count = sizes
    group, dp, place = (lax.axis_index(name) for name in ("groups", "dp", "tensor"))
    row, core = lax.div(dp, 2), lax.rem(dp, 2)
    width = tok_ref.shape[1]
    keeps = (
        pltpu.make_async_copy(tok_ref, columns(tok_out, place, width), local_sem.at[0]),
        pltpu.make_async_copy(staged, w_out.at[place], local_sem.at[1]),
    )
    loads = (
        pltpu.make_async_copy(w_ref, staged, local_sem.at[2]),
        pltpu.make_async_copy(got_ref, held, local_sem.at[3]),
    )
    keeps[0].start()
    for load in loads:
        load.start()
    other_groups = [lax.rem(group + hop, groups) for hop in range(groups)]
    other_rows = [lax.rem(row + hop, rows) for hop in range(rows)]
    sibling = {"dp": row * 2 + 1 - core}
    targets, conditions = line_targets(count, place)
    targets += [{"groups": g} for g in other_groups[1:]]
    targets += [{"dp": y * 2 + core} for y in other_rows[1:]] + [sibling]
    greet(targets, conditions + [None] * (groups + rows - 1))

    def at(group_at, row_at, core_at):
        return (group_at * rows + row_at) * 2 + core_at

    mine = at(group, row, core)
    others = [lax.rem(place + 1 + slot, count) for slot in range(count - 1)]
    stores = [
        pltpu.make_async_copy(held.at[index], w_out.at[index, mine], local_sem.at[4 + slot])
        for slot, index in enumerate(others)
    ]
    toks = Chain(
        count,
        place,
        PARTS,
        lambda part: parted(tok_ref, PARTS, part),
        lambda index, part: part_columns(tok_out, index, width, PARTS, part),
        tok_send,
        tok_recv,
    )

    def across(slot, hop, hop_row, outward):
        index = others[slot]
        sems = g_send.at[slot, hop - 1, hop_row], g_recv.at[slot, hop - 1, hop_row]
        block_row = other_rows[(rows - hop_row) % rows]
        there = w_out.at[index, at(group, block_row, core)]
        here = w_out.at[index, at(other_groups[groups - hop], block_row, core)]
        target = {"groups": other_groups[hop]}
        source = got_ref.at[index] if hop_row == 0 else there
        return remote(source, there if outward else here, *sems, target)

    def along(slot, hop_g, hop, outward):
        index = others[slot]
        sems = y_send.at[slot, hop_g, hop - 1], y_recv.at[slot, hop_g, hop - 1]
        block_group = other_groups[(groups - hop_g) % groups]
        there = w_out.at[index, at(block_group, row, core)]
        here = w_out.at[index, at(block_group, other_rows[rows - hop], core)]
        target = {"dp": other_rows[hop] * 2 + core}
        block = there if outward else here
        if hop_g == 0:
            return remote(got_ref.at[index], block, *sems, target)
        return remote(block, block, *sems, target)

    def beside(slot, hop_g, hop, outward):
        index = others[slot]
        sems = c_send.at[slot, hop_g, hop], c_recv.at[slot, hop_g, hop]
        block_group = other_groups[(groups - hop_g) % groups]
        block_row = other_rows[(rows - hop) % rows]
        there = w_out.at[index, at(block_group, block_row, core)]
        here = w_out.at[index, at(block_group, block_row, 1 - core)]
        block = there if outward else here
        if hop_g == 0 and hop == 0:
            return remote(got_ref.at[index], block, *sems, sibling)
        return remote(block, block, *sems, sibling)

    def rows_last(slot):
        return slot % 2 == 0

    def first(slot):
        for hop in range(1, groups):
            across(slot, hop, 0, True).start()
        for hop in range(1, rows):
            along(slot, 0, hop, True).start()
        beside(slot, 0, 0, True).start()

    def second(slot):
        for hop_g in range(1, groups):
            across(slot, hop_g, 0, False).wait_recv()
            if rows_last(slot):
                for hop in range(1, rows):
                    along(slot, hop_g, hop, True).start()
            beside(slot, hop_g, 0, True).start()
        for hop in range(1, rows):
            along(slot, 0, hop, False).wait_recv()
            if not rows_last(slot):
                for hop_g in range(1, groups):
                    across(slot, hop_g, hop, True).start()
            beside(slot, 0, hop, True).start()

    def third(slot):
        for hop_g in range(1, groups):
            for hop in range(1, rows):
                if rows_last(slot):
                    along(slot, hop_g, hop, False).wait_recv()
                else:
                    across(slot, hop_g, hop, False).wait_recv()
                beside(slot, hop_g, hop, True).start()

    def last(slot):
        for hop_g in range(groups):
            for hop in range(rows):
                beside(slot, hop_g, hop, False).wait_recv()
                beside(slot, hop_g, hop, True).wait_send()
                if hop_g and (hop == 0 or not rows_last(slot)):
                    across(slot, hop_g, hop, True).wait_send()
                if hop and (hop_g == 0 or rows_last(slot)):
                    along(slot, hop_g, hop, True).wait_send()

    toks.begin()
    for slot in range(count - 1):
        first(slot)
    for load in loads:
        load.wait()
    keeps[1].start()
    for store in stores:
        store.start()
    for step in range(count - 1):
        for part in range(PARTS):
            toks.receive(step, part)
        second(step)
        if step >= 1:
            third(step - 1)
    third(count - 2)
    for slot in range(count - 1):
        last(slot)
    toks.finish()
    for copy in (*keeps, *stores):
        copy.wait()


def plane(context, w_slices, gathered, groups, rows, count):
    slots = count - 1
    sems = [(2 * slots, PARTS), (slots, groups - 1, rows), (slots, groups, rows - 1)]
    sems.append((slots, groups, rows))
    return pl.pallas_call(
        functools.partial(plane_kernel, (groups, rows, count)),
        out_shape=(
            jax.ShapeDtypeStruct(
                (context.shape[0], context.shape[1] * count), context.dtype
            ),
            jax.ShapeDtypeStruct((count,) + w_slices.shape, w_slices.dtype),
        ),
        in_specs=[pl.BlockSpec(memory_space=pl.ANY)] * 3,
        out_specs=(pl.BlockSpec(memory_space=pl.ANY),) * 2,
        scratch_shapes=[pltpu.VMEM(w_slices.shape, w_slices.dtype), pltpu.VMEM(gathered.shape, w_slices.dtype), pltpu.SemaphoreType.DMA((3 + count,))]
        + [pltpu.SemaphoreType.DMA(shape) for shape in sems for _ in range(2)],
        compiler_params=pltpu.CompilerParams(
            collective_id=1, has_side_effects=True, vmem_limit_bytes=16 << 20
        ),
    )(context, w_slices, gathered)


def shards(
    tokens,
    ln_gain,
    w_query,
    w_key,
    w_value,
    w_out,
    final_gain,
    w_cross_key,
    w_cross_value,
    dec_query,
    grad_out,
    passage_query,
    passage_length,
):
    pass_dev, seq_len, part_width = tokens.shape
    local_cols = w_query.shape[1]
    local_heads = local_cols // HD
    score_scale = HD ** (-0.5)
    row_count = pass_dev * seq_len
    query_count = dec_query.shape[0]
    dec_len = dec_query.shape[1]
    groups, dp_count = lax.axis_size("groups"), lax.axis_size("dp")
    tensor_count = lax.axis_size("tensor")
    asked = lax.all_gather(jnp.stack([dec_query, grad_out]), "dp", axis=1, tiled=True)
    slices = groups * dp_count
    slice_rows = local_cols // slices
    slice_at = lax.axis_index("groups") * dp_count + lax.axis_index("dp")
    out_slice = lax.dynamic_slice_in_dim(w_out, slice_at * slice_rows, slice_rows, 0)
    gathered_in = line_gather(tokens.reshape(row_count, part_width), tensor_count, 0)
    out_slice, gathered_in = lax.optimization_barrier((out_slice, gathered_in))
    out_slice = lax.all_gather(out_slice, "tensor", axis=0, tiled=False)
    full_width = gathered_in.shape[1]
    inputs_f = gathered_in.reshape(row_count, full_width).astype(jnp.float32)
    normed = norm_rows(inputs_f, ln_gain).astype(jnp.bfloat16)

    def project(weight):
        return (
            jnp.dot(normed, weight, preferred_element_type=jnp.float32)
            .astype(jnp.bfloat16)
            .reshape(pass_dev, seq_len, local_heads, HD)
        )

    self_queries = project(w_query)
    self_keys = project(w_key)
    self_values = project(w_value)
    pass_start = lax.axis_index("dp") * pass_dev
    own_length = lax.dynamic_slice_in_dim(passage_length, pass_start, pass_dev)
    positions = jnp.arange(seq_len, dtype=jnp.int32)
    own_valid = positions[None, :] < own_length[:, None]
    scores = (
        jnp.einsum("pqhd,pkhd->phqk", self_queries, self_keys, preferred_element_type=jnp.float32)
        * score_scale
    )
    scores = jnp.where(own_valid[:, None, None, :], scores, blocked)
    row_peak = jnp.max(scores, axis=-1, keepdims=True)
    expd = jnp.where(own_valid[:, None, None, :], jnp.exp(scores - row_peak), 0.0)
    weights = (expd / jnp.sum(expd, axis=-1, keepdims=True)).astype(jnp.bfloat16)
    context = (
        jnp.einsum("phqk,pkhd->pqhd", weights, self_values, preferred_element_type=jnp.float32)
        .astype(jnp.bfloat16)
        .reshape(row_count, local_cols)
    )
    all_context, out_full = plane(
        context,
        w_out.reshape(slices, slice_rows, full_width),
        out_slice,
        groups,
        dp_count // 2,
        tensor_count,
    )
    out_full = out_full.reshape(tensor_count * local_cols, full_width)
    summed = jnp.dot(all_context, out_full, preferred_element_type=jnp.float32)
    encoded = norm_rows(inputs_f + summed, final_gain).astype(jnp.bfloat16)
    cross_keys = jnp.dot(encoded, w_cross_key, preferred_element_type=jnp.float32).astype(
        jnp.bfloat16
    )
    cross_values = jnp.dot(encoded, w_cross_value, preferred_element_type=jnp.float32).astype(
        jnp.bfloat16
    )
    own_query = lax.dynamic_slice_in_dim(passage_query[:, 0], pass_start, pass_dev)
    chosen = own_query[:, None] == jnp.arange(asked.shape[1], dtype=jnp.int32)[None, :]
    picked = jnp.sum(
        jnp.where(chosen[None, :, :, None, None], asked[:, None].astype(jnp.float32), 0.0), axis=2
    ).astype(jnp.bfloat16)
    picked = picked.reshape(2, pass_dev, dec_len, local_heads, HD)
    query_heads, out_grad = picked[0], picked[1]
    key_heads = cross_keys.reshape(pass_dev, seq_len, local_heads, HD)
    value_heads = cross_values.reshape(pass_dev, seq_len, local_heads, HD)
    key_ok = own_valid[:, None, None, :]
    cross_scores = (
        jnp.einsum("pihd,pthd->phit", query_heads, key_heads, preferred_element_type=jnp.float32)
        * score_scale
    )
    cross_scores = jnp.where(key_ok, cross_scores, blocked)
    own_peak = jnp.max(cross_scores, axis=-1, keepdims=True)
    own_exp = jnp.where(key_ok, jnp.exp(cross_scores - own_peak), 0.0)
    own_sum = jnp.sum(own_exp, axis=-1, keepdims=True)
    own_probs = own_exp / own_sum
    grad_probs = jnp.einsum(
        "pihd,pthd->phit", out_grad, value_heads, preferred_element_type=jnp.float32
    )
    own_delta = jnp.sum(own_probs * grad_probs, axis=-1, keepdims=True)
    stats = jnp.concatenate([own_peak, own_sum, own_delta], axis=-1)
    all_stats = lax.all_gather(stats, "dp", axis=0, tiled=True)
    own_low = own_probs.astype(jnp.bfloat16)
    centred = (own_probs * (grad_probs - own_delta)).astype(jnp.bfloat16)

    def over_keys(factor, heads):
        return jnp.einsum("phit,pthd->pihd", factor, heads, preferred_element_type=jnp.float32)

    partials = jnp.stack(
        [
            over_keys(own_low, value_heads),
            over_keys(centred, key_heads),
            over_keys(own_low, key_heads),
        ],
        axis=1,
    ).astype(jnp.bfloat16)
    partials = partials.reshape(pass_dev, 3, dec_len, local_cols)
    all_partials = lax.all_gather(partials, "dp", axis=0, tiled=True)
    pass_total = all_partials.shape[0]

    def shares(targets):
        owned = (targets[:, None] == passage_query[:, 0][None, :])[:, :, None, None]
        peaks = jnp.where(owned, all_stats[None, :, :, :, 0], blocked)
        top = jnp.max(peaks, axis=1, keepdims=True)
        raised = jnp.where(owned, jnp.exp(peaks - top) , 0.0)
        total = jnp.sum(raised * all_stats[None, :, :, :, 1], axis=1, keepdims=True)
        return raised, total, top

    _, own_total, own_top = shares(own_query)
    low = (
        own_exp * (jnp.exp(own_peak - own_top[:, 0, :, :, None]) / own_total[:, 0, :, :, None])
    ).astype(jnp.bfloat16)
    d_values = jnp.einsum(
        "phit,pihd->pthd", low, out_grad, preferred_element_type=jnp.float32
    ).astype(jnp.bfloat16).reshape(pass_dev, seq_len, local_cols)
    query_ids = lax.axis_index("dp") * query_count + jnp.arange(query_count, dtype=jnp.int32)
    raised, total, _ = shares(query_ids)
    share = raised * all_stats[None, :, :, :, 1] / total
    share = share.transpose(0, 1, 3, 2)[..., None]
    pieces = all_partials.astype(jnp.float32).reshape(
        1, pass_total, 3, dec_len, local_heads, HD
    )
    attended_heads = jnp.sum(share * pieces[:, :, 0], axis=1).astype(jnp.bfloat16)
    grad_heads = grad_out.reshape(query_count, dec_len, local_heads, HD)
    row_delta = jnp.sum(
        grad_heads.astype(jnp.float32) * attended_heads.astype(jnp.float32), axis=-1
    )
    shift = all_stats[None, :, :, :, 2].transpose(0, 1, 3, 2) - row_delta[:, None]
    query_term = jnp.sum(share * (pieces[:, :, 1] + shift[..., None] * pieces[:, :, 2]), axis=1)
    attended = attended_heads.reshape(query_count, dec_len, local_cols)
    d_query = (
        (query_term * score_scale).astype(jnp.bfloat16).reshape(query_count, dec_len, local_cols)
    )
    return (attended, d_query, d_values)


def solution(mesh):
    in_specs = (
        P(("groups", "dp"), None, "tensor"),
        P(),
        P(None, "tensor"),
        P(None, "tensor"),
        P(None, "tensor"),
        P("tensor", None),
        P(),
        P(None, "tensor"),
        P(None, "tensor"),
        P(("groups", "dp"), None, "tensor"),
        P(("groups", "dp"), None, "tensor"),
        P("groups", None),
        P("groups"),
    )
    out_specs = (
        P(("groups", "dp"), None, "tensor"),
        P(("groups", "dp"), None, "tensor"),
        P(("groups", "dp"), None, "tensor"),
    )
    return jax.shard_map(shards, mesh=mesh, in_specs=in_specs, out_specs=out_specs, check_vma=False)
```
